32 devices in a mesh: groups: 2 (over x), beam: 16 (over z, y, core).
Axes of the slice: x: 2, y: 2, z: 4, core: 2. Of those that a mesh axis runs over, the one named last changes fastest.
Arguments:
- transmission: float32 [2, 2, 512, 512], P('groups'), parts along dimension 0, may hold values from -1 to 1, as said below
- beams: int32 [16, 2], P('beam'), may hold values from -64 to 63
- phases: int32 [32, 16], replicated, may hold values from 0 to 63
- positions: int32 [32, 2], replicated, may hold values from 0 to 128
- owner: int32 [32], replicated, may hold values from 0 to 15, as said below
Outputs:
- patterns: float32 [128, 128, 128], P(('groups', 'beam')), parts along dimension 0
The draws below stay inside these ranges and needn't reach their ends.
There are 2 independent parts, one for each index of `groups`. The reference program is written for one: setup_inputs(seed, part) draws one part's arguments, and reference() takes and returns one part's arrays. A program takes and returns all parts, laid end to end along the dimension named above; an argument that names none is the same for every part. Nothing has to cross between parts.
Inputs may be any that keep to these rules, and one draw needn't show every extreme that they name: `transmission`: real and imaginary parts of each pixel form a pair of magnitude at most 1. Each owner is given at most 4 probes, and some owner exactly 4.
All inputs are finite; a program needn't handle non-finite values.
Results may differ from the reference program's by a relative error of at most 0.0003.
Values sent between devices are 32-bit elements; how exact they have to be, the bound alone decides.
A program may use at most 64 MiB of HBM per device.

```python
import math
import jax
import jax.numpy as jnp
from jax import lax

GRID = 512
CROP = 256
WINDOW = 128
SLICES = 1
LEVELS = 64
BEAMS = 16
PROBES = 32
CAP = 4
SLOTS = 64


def draw_transmission(key, part):
    key_amp, key_angle = jax.random.split(key, 2)
    array_shape = (SLICES, GRID, GRID)
    magnitude = jax.random.uniform(key_amp, array_shape, jnp.float32, 0.6, 1.0)
    phase_angle = jax.random.uniform(key_angle, array_shape, jnp.float32, -math.pi, math.pi)
    return jnp.stack([magnitude * jnp.cos(phase_angle), magnitude * jnp.sin(phase_angle)], axis=1).astype(jnp.float32)


def draw_owner(key, part):
    key_perm, key_full, key_order = jax.random.split(key, 3)
    owners_total = SLOTS // CAP
    shuffled_slots = jax.random.permutation(key_perm, SLOTS)
    full_owner = jax.random.randint(key_full, (), 0, owners_total)
    priority = jnp.where(shuffled_slots // CAP == full_owner, 0, SLOTS) + jnp.arange(SLOTS)
    chosen = shuffled_slots[jnp.argsort(priority)][:PROBES]
    mixed = chosen[jax.random.permutation(key_order, PROBES)]
    return (mixed // CAP).astype(jnp.int32)


def with_ends(entries, own_key, smallest, top_value):
    index_at = [jax.random.randint(jax.random.fold_in(own_key, axis), (), 0, length) for axis, length in enumerate(entries.shape)]
    longest = entries.shape.index(max(entries.shape))
    beside = index_at[:longest] + [(index_at[longest] + 1) % entries.shape[longest]] + index_at[longest + 1:]
    return entries.at[tuple(index_at)].set(smallest).at[tuple(beside)].set(top_value)


def setup_inputs(seed: int = 0, part: int = 0) -> dict:
    arg_keys = jax.random.split(jax.random.key(seed), 6)
    part_keys = jax.random.split(jax.random.fold_in(arg_keys[5], part), 6)
    return {
        "transmission": draw_transmission(jax.random.fold_in(jax.random.fold_in(arg_keys[5], part), 71), part),
        "beams": with_ends(jax.random.randint(arg_keys[1], (BEAMS, 2), 0 - GRID // 8, GRID // 8), jax.random.fold_in(arg_keys[1], 1), 0 - GRID // 8, (GRID // 8) - 1).astype(jnp.int32),
        "phases": with_ends(jax.random.randint(arg_keys[2], (PROBES, BEAMS), 0, LEVELS), jax.random.fold_in(arg_keys[2], 1), 0, LEVELS - 1).astype(jnp.int32),
        "positions": with_ends(jax.random.randint(arg_keys[3], (PROBES, 2), 0, CROP - WINDOW + 1), jax.random.fold_in(arg_keys[3], 1), 0, CROP - WINDOW).astype(jnp.int32),
        "owner": draw_owner(jax.random.fold_in(arg_keys[5], 71), part),
    }


highest = lax.Precision.HIGHEST
prop_rate = 0.0004 * math.pi
two_pi = 2.0 * math.pi

def reference(transmission, beams, phases, positions, owner):
    index = jnp.arange(GRID, dtype=jnp.int32)
    signed = jnp.where(index < GRID // 2, index, index - GRID)
    prop_angle = (signed[:, None] * signed[:, None] + signed[None, :] * signed[None, :]).astype(jnp.float32) * prop_rate
    propagate = lax.complex(jnp.cos(prop_angle), -jnp.sin(prop_angle))
    lower = (GRID - CROP) // 2

    def one_beam(beam_pair):
        angles = ((beam_pair[0] * index[:, None] + beam_pair[1] * index[None, :]) % GRID).astype(jnp.float32) * (two_pi / GRID)
        wave = lax.complex(jnp.cos(angles), jnp.sin(angles))
        for slice_index in range(SLICES):
            specimen = lax.complex(transmission[slice_index, 0], transmission[slice_index, 1])
            wave = jnp.fft.ifft2(jnp.fft.fft2(specimen * wave) * propagate)
        cropped = wave[lower:lower + CROP, lower:lower + CROP]
        return jnp.stack([jnp.real(cropped), jnp.imag(cropped)])
    exits = lax.map(one_beam, beams)
    beam_total = beams.shape[0]
    weight_angle = phases.astype(jnp.float32) * (two_pi / LEVELS)
    weight_real = jnp.cos(weight_angle) / math.sqrt(beam_total)
    weight_imag = jnp.sin(weight_angle) / math.sqrt(beam_total)

    def one_probe(inputs):
        real_weight, imag_weight, offset = inputs
        window = lax.dynamic_slice(exits, (jnp.int32(0), jnp.int32(0), offset[0], offset[1]), (beam_total, 2, WINDOW, WINDOW))
        real_sum = jnp.einsum('b,byx->yx', real_weight, window[:, 0], precision=highest) - jnp.einsum('b,byx->yx', imag_weight, window[:, 1], precision=highest)
        imag_sum = jnp.einsum('b,byx->yx', real_weight, window[:, 1], precision=highest) + jnp.einsum('b,byx->yx', imag_weight, window[:, 0], precision=highest)
        spectrum = jnp.fft.fft2(lax.complex(real_sum, imag_sum))
        return (jnp.real(spectrum) * jnp.real(spectrum) + jnp.imag(spectrum) * jnp.imag(spectrum)) / (WINDOW * WINDOW)
    powers = lax.map(one_probe, (weight_real, weight_imag, positions))
    probe_ids = jnp.arange(PROBES, dtype=jnp.int32)
    same_owner = owner[:, None] == owner[None, :]
    earlier = probe_ids[None, :] < probe_ids[:, None]
    rank = lax.optimization_barrier(jnp.sum(jnp.where(same_owner & earlier, 1, 0), axis=1)).astype(jnp.int32)
    target = owner * CAP + rank
    return jnp.zeros((SLOTS, WINDOW, WINDOW), jnp.float32).at[target].set(powers.astype(jnp.float32))
```

```python
import functools
import math

import jax
import jax.numpy as jnp
import ml_dtypes
import numpy as np
from jax import lax
from jax.experimental import pallas as pl
from jax.experimental.pallas import tpu as pltpu
from jax.sharding import PartitionSpec as P

GRID = 512
CROP = 256
WINDOW = 128
LEVELS = 64
CAP = 4
TEAM = 8
CHUNK = 16

bf16 = jnp.bfloat16
f32 = jnp.float32
MESH = pl.DeviceIdType.MESH


def host_split(x):
    x = np.asarray(x, np.float32)
    hi = x.astype(ml_dtypes.bfloat16)
    lo = (x - hi.astype(np.float32)).astype(ml_dtypes.bfloat16)
    return hi, lo


def constants(length, team):
    index = np.arange(length)
    freq = np.where(index < length // 2, index, index - length)
    chirp = np.exp(-1j * 0.0004 * np.pi * freq.astype(np.float64) ** 2)
    kernel = np.fft.ifft(chirp)
    rows = (length - CROP) // 2 + np.arange(CROP)
    step = kernel[(rows[:, None] - index[None, :]) % length]
    dealt = step.reshape(CROP // team, team, length).transpose(1, 0, 2)
    a = np.stack([dealt.real, dealt.imag], axis=1).astype(np.float32)
    st = step.T
    b = np.block([[st.real, st.imag], [-st.imag, st.real]])
    w = np.arange(WINDOW)
    ang = 2 * np.pi * ((w[:, None] * w[None, :]) % WINDOW) / WINDOW
    c, s = np.cos(ang), np.sin(ang)
    x = np.block([[c, -s], [s, c]])
    order = w.reshape(WINDOW // team, team).T.reshape(-1)
    y = np.concatenate([c[:, order], s[:, order]], axis=0)
    return a, host_split(b), host_split(x), host_split(y)


def split(x):
    hi = x.astype(bf16)
    return hi, (x - hi.astype(f32)).astype(bf16)


def dot(a, b):
    return jnp.dot(a, b, preferred_element_type=f32)


def dot3(ah, al, bh, bl):
    return dot(ah, bh) + (dot(ah, bl) + dot(al, bh))


def kernel(n, team, chunk,
           t_ref, beams_ref, phases_ref, pos_ref, owner_ref, a_ref, bh_ref, bl_ref,
           xh_ref, xl_ref, yh_ref, yl_ref, out_ref,
           kmine, kbuf, th, tl, lh, ll, s_buf, eh, el, wh, wl, p_buf, xbuf, zbuf,
           ksend, krecv, xsend, xrecv):
    length = t_ref.shape[1]
    probes, beams = phases_ref.shape
    hold = CROP // team
    fold = WINDOW // team
    m = chunk * hold
    slots = team * CAP
    sj = slots * fold
    me = lax.axis_index("beam")
    mi = lax.rem(me, team)
    base = me - mi

    barrier = pltpu.get_barrier_semaphore()
    for d in range(1, n):
        pl.semaphore_signal(barrier, inc=1, device_id={"beam": lax.rem(me + d, n)}, device_id_type=MESH)
    half = lax.broadcasted_iota(jnp.int32, (8, 128), 0) < 4
    kmine[...] = jnp.where(half, beams_ref[0:1, 0:1], beams_ref[0:1, 1:2])
    kbuf[me] = kmine[...]
    pl.semaphore_wait(barrier, n - 1)
    sends = []
    for d in range(1, n):
        copy = pltpu.make_async_remote_copy(
            src_ref=kmine, dst_ref=kbuf.at[me], send_sem=ksend.at[d - 1], recv_sem=krecv.at[d - 1],
            device_id={"beam": lax.rem(me + d, n)}, device_id_type=MESH)
        copy.start()
        sends.append(copy)

    t_hi, t_lo = split(t_ref[...])
    th[...] = t_hi
    tl[...] = t_lo
    owner_row = owner_ref[...].astype(f32)
    pi = lax.broadcasted_iota(jnp.int32, (probes, probes), 0)
    pj = lax.broadcasted_iota(jnp.int32, (probes, probes), 1)
    owner_col = jnp.sum(jnp.where(pi == pj, owner_row, 0.0), axis=1, keepdims=True)
    rank = jnp.sum(jnp.where((owner_col == owner_row) & (pi < pj), 1.0, 0.0), axis=0, keepdims=True)
    target = owner_row * CAP + rank
    slot_id = (lax.broadcasted_iota(jnp.int32, (slots, probes), 0) + base * CAP).astype(f32)
    hit = jnp.where(target == slot_id, 1.0, 0.0)
    used = jnp.sum(hit, axis=1, keepdims=True)
    hit16 = hit.astype(bf16)
    place = dot(hit16, pos_ref[...].astype(f32).astype(bf16))
    level = dot(hit16, phases_ref[...].astype(f32).astype(bf16)).astype(bf16)

    def rows_of(x):
        return jnp.broadcast_to(x[:, None, :], (slots, fold, x.shape[-1])).reshape(sj, x.shape[-1])

    top = rows_of(jnp.broadcast_to(place[:, 0:1], (slots, 128)))[:, 0:1]
    left = rows_of(jnp.broadcast_to(place[:, 1:2], (slots, 128)))
    j_row = lax.broadcasted_iota(jnp.int32, (sj, 1), 0) & (fold - 1)
    first = (j_row * team + mi).astype(f32)
    pick = j_row + jnp.where(first < top, fold, 0)

    for copy in sends:
        copy.wait_recv()

    def one_chunk(c, is_first):
        bi = lax.broadcasted_iota(jnp.int32, (beams, m), 0)
        bj = lax.broadcasted_iota(jnp.int32, (beams, m), 1)
        spread = jnp.where(bi == c * chunk + bj // hold, 1.0, 0.0).astype(bf16)
        angle = dot(level, spread) * (2.0 * math.pi / LEVELS)
        scale = used * (1.0 / math.sqrt(beams))
        keep = (lax.broadcasted_iota(jnp.int32, (sj, m), 1) & (hold - 1)) == pick
        w_hi, w_lo = split(jnp.where(keep, rows_of(jnp.cos(angle) * scale), 0.0))
        wh[0:sj] = w_hi
        wl[0:sj] = w_lo
        w_hi, w_lo = split(jnp.where(keep, rows_of(jnp.sin(angle) * scale), 0.0))
        wh[sj:] = w_hi
        wl[sj:] = w_lo

        index = lax.broadcasted_iota(jnp.int32, (chunk, length), 1)

        def wave(row):
            k = kbuf[pl.ds(c * chunk, chunk), row, :]
            k = jnp.concatenate([k] * (length // 128), axis=1)
            ang = ((k * index) & (length - 1)).astype(f32) * (2.0 * math.pi / length)
            return jnp.cos(ang)[:, None, :], jnp.sin(ang)[:, None, :]

        cy, sy = wave(0)
        cx, sx = wave(4)
        ar = a_ref[mi, 0][None]
        ai = a_ref[mi, 1][None]
        lr_hi, lr_lo = split((ar * cy - ai * sy).reshape(m, length))
        li_hi, li_lo = split((ar * sy + ai * cy).reshape(m, length))
        lh[0:m, 0:length] = lr_hi
        ll[0:m, 0:length] = lr_lo
        lh[0:m, length:] = -li_hi
        ll[0:m, length:] = -li_lo
        lh[m:, 0:length] = li_hi
        ll[m:, 0:length] = li_lo
        lh[m:, length:] = lr_hi
        ll[m:, length:] = lr_lo

        @pl.loop(0, length // 256)
        def _(q):
            cols = pl.ds(pl.multiple_of(q * 256, 256), 256)
            s_buf[:, cols] = dot3(lh[...], ll[...], th[:, cols], tl[:, cols])

        sr = s_buf[0:m].reshape(chunk, hold, length)
        si = s_buf[m:].reshape(chunk, hold, length)
        hi, lo = split((sr * cx - si * sx).reshape(m, length))
        lh[0:m, 0:length] = hi
        ll[0:m, 0:length] = lo
        hi, lo = split((sr * sx + si * cx).reshape(m, length))
        lh[0:m, length:] = hi
        ll[0:m, length:] = lo

        @pl.loop(0, 2 * CROP // 256)
        def _(q):
            cols = pl.ds(pl.multiple_of(q * 256, 256), 256)
            hi, lo = split(dot3(lh[0:m], ll[0:m], bh_ref[:, cols], bl_ref[:, cols]))
            eh[:, cols] = hi
            el[:, cols] = lo

        @pl.loop(0, 2 * CROP // 256)
        def _(q):
            cols = pl.ds(pl.multiple_of(q * 256, 256), 256)
            part = dot3(wh[...], wl[...], eh[:, cols], el[:, cols])
            p_buf[:, cols] = part if is_first else p_buf[:, cols] + part

    one_chunk(0, True)
    if beams > chunk:
        @pl.loop(1, beams // chunk)
        def _(c):
            one_chunk(c, False)

    vr = p_buf[0:sj, 0:CROP] - p_buf[sj:, CROP:]
    vi = p_buf[0:sj, CROP:] + p_buf[sj:, 0:CROP]
    inside = lax.broadcasted_iota(jnp.int32, (sj, WINDOW), 1).astype(f32) >= left
    folded = jnp.concatenate(
        [jnp.where(inside, vr[:, 0:WINDOW], vr[:, WINDOW:]),
         jnp.where(inside, vi[:, 0:WINDOW], vi[:, WINDOW:])], axis=1)
    f_hi, f_lo = split(folded)
    xbuf[...] = dot3(f_hi, f_lo, xh_ref[...], xl_ref[...]).reshape(team, CAP * fold, 2 * WINDOW)

    copies = []
    for e in range(1, team):
        other = lax.rem(mi + e, team)
        copy = pltpu.make_async_remote_copy(
            src_ref=xbuf.at[other], dst_ref=zbuf.at[mi], send_sem=xsend.at[e - 1], recv_sem=xrecv.at[e - 1],
            device_id={"beam": base + other}, device_id_type=MESH)
        copy.start()
        copies.append(copy)
    zbuf[mi] = xbuf[mi]
    for copy in copies:
        copy.wait_recv()
    for k in range(CAP):
        z = zbuf[:, k * fold:(k + 1) * fold, :].reshape(WINDOW, 2 * WINDOW)
        z_hi, z_lo = split(z)
        y = dot3(yh_ref[...], yl_ref[...], z_hi, z_lo)
        yr = y[0:WINDOW, 0:WINDOW] + y[WINDOW:, WINDOW:]
        yi = y[0:WINDOW, WINDOW:] - y[WINDOW:, 0:WINDOW]
        out_ref[k] = (yr * yr + yi * yi) * (1.0 / (WINDOW * WINDOW))
    for copy in sends + copies:
        copy.wait_send()


def solution(mesh):
    n = mesh.shape["beam"]
    team = math.gcd(n, TEAM)

    def local(transmission, beams, phases, positions, owner):
        length = transmission.shape[-1]
        probes, beam_total = phases.shape
        chunk = math.gcd(beam_total, CHUNK)
        a, b, x, y = constants(length, team)
        m = chunk * (CROP // team)
        sj = CAP * WINDOW
        t = transmission.reshape(2 * length, length)
        return pl.pallas_call(
            functools.partial(kernel, n, team, chunk),
            out_shape=jax.ShapeDtypeStruct((CAP, WINDOW, WINDOW), f32),
            in_specs=[pl.BlockSpec(memory_space=pltpu.VMEM)] * 12,
            out_specs=pl.BlockSpec(memory_space=pltpu.VMEM),
            scratch_shapes=[
                pltpu.VMEM((8, 128), jnp.int32),
                pltpu.VMEM((n, 8, 128), jnp.int32),
                pltpu.VMEM((2 * length, length), bf16),
                pltpu.VMEM((2 * length, length), bf16),
                pltpu.VMEM((2 * m, 2 * length), bf16),
                pltpu.VMEM((2 * m, 2 * length), bf16),
                pltpu.VMEM((2 * m, length), f32),
                pltpu.VMEM((m, 2 * CROP), bf16),
                pltpu.VMEM((m, 2 * CROP), bf16),
                pltpu.VMEM((2 * sj, m), bf16),
                pltpu.VMEM((2 * sj, m), bf16),
                pltpu.VMEM((2 * sj, 2 * CROP), f32),
                pltpu.VMEM((team, CAP * WINDOW // team, 2 * WINDOW), f32),
                pltpu.VMEM((team, CAP * WINDOW // team, 2 * WINDOW), f32),
                pltpu.SemaphoreType.DMA((n - 1,)),
                pltpu.SemaphoreType.DMA((n - 1,)),
                pltpu.SemaphoreType.DMA((team - 1,)),
                pltpu.SemaphoreType.DMA((team - 1,)),
            ],
            compiler_params=pltpu.CompilerParams(
                collective_id=0, has_side_effects=True, vmem_limit_bytes=48 << 20),
        )(t, beams, phases, positions, owner.reshape(1, probes), a, *b, *x, *y)

    in_specs = (P("groups", None, None, None), P("beam", None), P(), P(), P())
    out_specs = P(("groups", "beam"), None, None)
    return jax.shard_map(local, mesh=mesh, in_specs=in_specs, out_specs=out_specs, check_vma=False)
```

```python
import functools
import math

import jax
import jax.numpy as jnp
import ml_dtypes
import numpy as np
from jax import lax
from jax.experimental import pallas as pl
from jax.experimental.pallas import tpu as pltpu
from jax.sharding import PartitionSpec as P

GRID = 512
CROP = 256
WINDOW = 128
LEVELS = 64
CAP = 4
TEAM = 8
CHUNK = 16

bf16 = jnp.bfloat16
f32 = jnp.float32
MESH = pl.DeviceIdType.MESH


def host_split(x):
    x = np.asarray(x, np.float32)
    hi = x.astype(ml_dtypes.bfloat16)
    lo = (x - hi.astype(np.float32)).astype(ml_dtypes.bfloat16)
    return hi, lo


def constants(length, team):
    index = np.arange(length)
    freq = np.where(index < length // 2, index, index - length)
    chirp = np.exp(-1j * 0.0004 * np.pi * freq.astype(np.float64) ** 2)
    kernel = np.fft.ifft(chirp)
    rows = (length - CROP) // 2 + np.arange(CROP)
    step = kernel[(rows[:, None] - index[None, :]) % length]
    dealt = step.reshape(CROP // team, team, length).transpose(1, 0, 2)
    a = np.stack([dealt.real, dealt.imag], axis=1).astype(np.float32)
    st = step.T
    b = np.block([[st.real, st.imag], [-st.imag, st.real]])
    w = np.arange(WINDOW)
    ang = 2 * np.pi * ((w[:, None] * w[None, :]) % WINDOW) / WINDOW
    c, s = np.cos(ang), np.sin(ang)
    x = np.block([[c, -s], [s, c]])
    order = w.reshape(WINDOW // team, team).T.reshape(-1)
    y = np.concatenate([c[:, order], s[:, order]], axis=0)
    return a, host_split(b), host_split(x), host_split(y)


def split(x):
    hi = x.astype(bf16)
    return hi, (x - hi.astype(f32)).astype(bf16)


def dot(a, b):
    return jnp.dot(a, b, preferred_element_type=f32)


def dot_t(a, b):
    return lax.dot_general(a, b, (((1,), (1,)), ((), ())), preferred_element_type=f32)


def dot3(ah, al, bh, bl):
    return dot(ah, bh) + (dot(ah, bl) + dot(al, bh))


def kernel(n, team, chunk,
           t_hbm, beams_hbm, phases_hbm, pos_hbm, owner_hbm, a_hbm, bh_hbm, bl_hbm,
           xh_hbm, xl_hbm, yh_hbm, yl_hbm, out_ref,
           t_ref, beams_ref, phases_ref, pos_ref, owner_ref, a_ref, bh_ref, bl_ref,
           xh_ref, xl_ref, yh_ref, yl_ref, fetch,
           kmine, kbuf, th, tl, lh, ll, s_buf, eh, el, wh, wl, p_buf, xbuf, zbuf,
           ksend, krecv, xsend, xrecv):
    length = t_ref.shape[1]
    beams, probes = phases_ref.shape
    hold = CROP // team
    fold = WINDOW // team
    m = chunk * hold
    slots = team * CAP
    sj = slots * fold
    me = lax.axis_index("beam")
    mi = lax.rem(me, team)
    base = me - mi

    moves = [
        pltpu.make_async_copy(src, dst, fetch.at[i]) for i, (src, dst) in enumerate((
            (beams_hbm, beams_ref), (owner_hbm, owner_ref), (phases_hbm, phases_ref), (pos_hbm, pos_ref),
            (t_hbm, t_ref), (a_hbm.at[mi], a_ref), (bh_hbm, bh_ref), (bl_hbm, bl_ref),
            (xh_hbm, xh_ref), (xl_hbm, xl_ref), (yh_hbm, yh_ref), (yl_hbm, yl_ref)))]
    for move in moves:
        move.start()
    barrier = pltpu.get_barrier_semaphore()
    for d in range(1, n):
        pl.semaphore_signal(barrier, inc=1, device_id={"beam": lax.rem(me + d, n)}, device_id_type=MESH)
    moves[0].wait()
    half = lax.broadcasted_iota(jnp.int32, (8, 128), 0) < 4
    kmine[...] = jnp.where(half, beams_ref[0:1, 0:1], beams_ref[0:1, 1:2])
    kbuf[me] = kmine[...]
    pl.semaphore_wait(barrier, n - 1)
    sends = []
    for d in range(1, n):
        copy = pltpu.make_async_remote_copy(
            src_ref=kmine, dst_ref=kbuf.at[me], send_sem=ksend.at[d - 1], recv_sem=krecv.at[d - 1],
            device_id={"beam": lax.rem(me + d, n)}, device_id_type=MESH)
        copy.start()
        sends.append(copy)

    for move in moves[1:4]:
        move.wait()
    owner_row = owner_ref[...].astype(f32)
    pi = lax.broadcasted_iota(jnp.int32, (probes, probes), 0)
    pj = lax.broadcasted_iota(jnp.int32, (probes, probes), 1)
    owner_col = jnp.sum(jnp.where(pi == pj, owner_row, 0.0), axis=1, keepdims=True)
    rank = jnp.sum(jnp.where((owner_col == owner_row) & (pi < pj), 1.0, 0.0), axis=0, keepdims=True)
    target = owner_row * CAP + rank
    slot_id = (lax.broadcasted_iota(jnp.int32, (slots, probes), 0) + base * CAP).astype(f32)
    hit = jnp.where(target == slot_id, 1.0, 0.0)
    used = jnp.sum(hit, axis=1, keepdims=True)
    hit16 = hit.astype(bf16)
    place = dot_t(hit16, pos_ref[...].astype(f32).astype(bf16))
    level = dot_t(hit16, phases_ref[...].astype(f32).astype(bf16)).astype(bf16)

    def rows_of(x):
        return jnp.broadcast_to(x[:, None, :], (slots, fold, x.shape[-1])).reshape(sj, x.shape[-1])

    top = rows_of(jnp.broadcast_to(place[:, 0:1], (slots, 128)))[:, 0:1]
    left = rows_of(jnp.broadcast_to(place[:, 1:2], (slots, 128)))
    j_row = lax.broadcasted_iota(jnp.int32, (sj, 1), 0) & (fold - 1)
    first = (j_row * team + mi).astype(f32)
    pick = j_row + jnp.where(first < top, fold, 0)

    moves[4].wait()
    t_hi, t_lo = split(t_ref[...])
    th[...] = t_hi
    tl[...] = t_lo
    for move in moves[5:]:
        move.wait()
    for copy in sends:
        copy.wait_recv()

    def one_chunk(c, is_first):
        bi = lax.broadcasted_iota(jnp.int32, (beams, m), 0)
        bj = lax.broadcasted_iota(jnp.int32, (beams, m), 1)
        spread = jnp.where(bi == c * chunk + bj // hold, 1.0, 0.0).astype(bf16)
        angle = dot(level, spread) * (2.0 * math.pi / LEVELS)
        scale = used * (1.0 / math.sqrt(beams))
        keep = (lax.broadcasted_iota(jnp.int32, (sj, m), 1) & (hold - 1)) == pick
        w_hi, w_lo = split(jnp.where(keep, rows_of(jnp.cos(angle) * scale), 0.0))
        wh[0:sj] = w_hi
        wl[0:sj] = w_lo
        w_hi, w_lo = split(jnp.where(keep, rows_of(jnp.sin(angle) * scale), 0.0))
        wh[sj:] = w_hi
        wl[sj:] = w_lo

        index = lax.broadcasted_iota(jnp.int32, (chunk, length), 1)

        def wave(row):
            k = kbuf[pl.ds(c * chunk, chunk), row, :]
            k = jnp.concatenate([k] * (length // 128), axis=1)
            ang = ((k * index) & (length - 1)).astype(f32) * (2.0 * math.pi / length)
            return jnp.cos(ang)[:, None, :], jnp.sin(ang)[:, None, :]

        cy, sy = wave(0)
        cx, sx = wave(4)
        ar = a_ref[0][None]
        ai = a_ref[1][None]
        lr_hi, lr_lo = split((ar * cy - ai * sy).reshape(m, length))
        li_hi, li_lo = split((ar * sy + ai * cy).reshape(m, length))
        lh[0:m, 0:length] = lr_hi
        ll[0:m, 0:length] = lr_lo
        lh[0:m, length:] = -li_hi
        ll[0:m, length:] = -li_lo
        lh[m:, 0:length] = li_hi
        ll[m:, 0:length] = li_lo
        lh[m:, length:] = lr_hi
        ll[m:, length:] = lr_lo

        @pl.loop(0, length // 256)
        def _(q):
            cols = pl.ds(pl.multiple_of(q * 256, 256), 256)
            s_buf[:, cols] = dot3(lh[...], ll[...], th[:, cols], tl[:, cols])

        sr = s_buf[0:m].reshape(chunk, hold, length)
        si = s_buf[m:].reshape(chunk, hold, length)
        hi, lo = split((sr * cx - si * sx).reshape(m, length))
        lh[0:m, 0:length] = hi
        ll[0:m, 0:length] = lo
        hi, lo = split((sr * sx + si * cx).reshape(m, length))
        lh[0:m, length:] = hi
        ll[0:m, length:] = lo

        @pl.loop(0, 2 * CROP // 256)
        def _(q):
            cols = pl.ds(pl.multiple_of(q * 256, 256), 256)
            hi, lo = split(dot3(lh[0:m], ll[0:m], bh_ref[:, cols], bl_ref[:, cols]))
            eh[:, cols] = hi
            el[:, cols] = lo

        @pl.loop(0, 2 * CROP // 256)
        def _(q):
            cols = pl.ds(pl.multiple_of(q * 256, 256), 256)
            part = dot3(wh[...], wl[...], eh[:, cols], el[:, cols])
            p_buf[:, cols] = part if is_first else p_buf[:, cols] + part

    one_chunk(0, True)
    if beams > chunk:
        @pl.loop(1, beams // chunk)
        def _(c):
            one_chunk(c, False)

    vr = p_buf[0:sj, 0:CROP] - p_buf[sj:, CROP:]
    vi = p_buf[0:sj, CROP:] + p_buf[sj:, 0:CROP]
    inside = lax.broadcasted_iota(jnp.int32, (sj, WINDOW), 1).astype(f32) >= left
    folded = jnp.concatenate(
        [jnp.where(inside, vr[:, 0:WINDOW], vr[:, WINDOW:]),
         jnp.where(inside, vi[:, 0:WINDOW], vi[:, WINDOW:])], axis=1)
    f_hi, f_lo = split(folded)
    xbuf[...] = dot3(f_hi, f_lo, xh_ref[...], xl_ref[...]).reshape(team, CAP * fold, 2 * WINDOW)

    copies = []
    for e in range(1, team):
        other = lax.rem(mi + e, team)
        copy = pltpu.make_async_remote_copy(
            src_ref=xbuf.at[other], dst_ref=zbuf.at[mi], send_sem=xsend.at[e - 1], recv_sem=xrecv.at[e - 1],
            device_id={"beam": base + other}, device_id_type=MESH)
        copy.start()
        copies.append(copy)
    zbuf[mi] = xbuf[mi]
    for copy in copies:
        copy.wait_recv()
    for k in range(CAP):
        z = zbuf[:, k * fold:(k + 1) * fold, :].reshape(WINDOW, 2 * WINDOW)
        z_hi, z_lo = split(z)
        y = dot3(yh_ref[...], yl_ref[...], z_hi, z_lo)
        yr = y[0:WINDOW, 0:WINDOW] + y[WINDOW:, WINDOW:]
        yi = y[0:WINDOW, WINDOW:] - y[WINDOW:, 0:WINDOW]
        out_ref[k] = (yr * yr + yi * yi) * (1.0 / (WINDOW * WINDOW))
    for copy in sends + copies:
        copy.wait_send()


def solution(mesh):
    n = mesh.shape["beam"]
    team = math.gcd(n, TEAM)

    def local(transmission, beams, phases, positions, owner):
        length = transmission.shape[-1]
        probes, beam_total = phases.shape
        chunk = math.gcd(beam_total, CHUNK)
        a, b, x, y = constants(length, team)
        m = chunk * (CROP // team)
        sj = CAP * WINDOW
        t = transmission.reshape(2 * length, length)
        operands = (t, beams, phases.T, positions.T, owner.reshape(1, probes), a, *b, *x, *y)
        held = [pltpu.VMEM(v.shape[1:] if v is a else v.shape, v.dtype) for v in operands]
        return pl.pallas_call(
            functools.partial(kernel, n, team, chunk),
            out_shape=jax.ShapeDtypeStruct((CAP, WINDOW, WINDOW), f32),
            in_specs=[pl.BlockSpec(memory_space=pl.ANY)] * 12,
            out_specs=pl.BlockSpec(memory_space=pltpu.VMEM),
            scratch_shapes=held + [
                pltpu.SemaphoreType.DMA((len(operands),)),
                pltpu.VMEM((8, 128), jnp.int32),
                pltpu.VMEM((n, 8, 128), jnp.int32),
                pltpu.VMEM((2 * length, length), bf16),
                pltpu.VMEM((2 * length, length), bf16),
                pltpu.VMEM((2 * m, 2 * length), bf16),
                pltpu.VMEM((2 * m, 2 * length), bf16),
                pltpu.VMEM((2 * m, length), f32),
                pltpu.VMEM((m, 2 * CROP), bf16),
                pltpu.VMEM((m, 2 * CROP), bf16),
                pltpu.VMEM((2 * sj, m), bf16),
                pltpu.VMEM((2 * sj, m), bf16),
                pltpu.VMEM((2 * sj, 2 * CROP), f32),
                pltpu.VMEM((team, CAP * WINDOW // team, 2 * WINDOW), f32),
                pltpu.VMEM((team, CAP * WINDOW // team, 2 * WINDOW), f32),
                pltpu.SemaphoreType.DMA((n - 1,)),
                pltpu.SemaphoreType.DMA((n - 1,)),
                pltpu.SemaphoreType.DMA((team - 1,)),
                pltpu.SemaphoreType.DMA((team - 1,)),
            ],
            compiler_params=pltpu.CompilerParams(
                collective_id=0, has_side_effects=True, vmem_limit_bytes=60 << 20),
        )(*operands)

    in_specs = (P("groups", None, None, None), P("beam", None), P(), P(), P())
    out_specs = P(("groups", "beam"), None, None)
    return jax.shard_map(local, mesh=mesh, in_specs=in_specs, out_specs=out_specs, check_vma=False)
```

```python
import functools
import math

import jax
import jax.numpy as jnp
import ml_dtypes
import numpy as np
from jax import lax
from jax.experimental import pallas as pl
from jax.experimental.pallas import tpu as pltpu
from jax.sharding import PartitionSpec as P

GRID = 512
CROP = 256
WINDOW = 128
LEVELS = 64
CAP = 4
TEAM = 8
CHUNK = 16
PARTS = 2

bf16 = jnp.bfloat16
f32 = jnp.float32
MESH = pl.DeviceIdType.MESH


def host_split(x):
    x = np.asarray(x, np.float32)
    hi = x.astype(ml_dtypes.bfloat16)
    lo = (x - hi.astype(np.float32)).astype(ml_dtypes.bfloat16)
    return hi, lo


def constants(length, team):
    index = np.arange(length)
    freq = np.where(index < length // 2, index, index - length)
    chirp = np.exp(-1j * 0.0004 * np.pi * freq.astype(np.float64) ** 2)
    kernel = np.fft.ifft(chirp)
    rows = (length - CROP) // 2 + np.arange(CROP)
    step = kernel[(rows[:, None] - index[None, :]) % length]
    fp = WINDOW // team // PARTS
    dealt = step.reshape(2, PARTS, fp, team, length).transpose(3, 1, 0, 2, 4).reshape(team, PARTS, 2 * fp, length)
    a = np.stack([dealt.real, dealt.imag], axis=2).astype(np.float32)
    st = step.T
    b = np.block([[st.real, st.imag], [-st.imag, st.real]])
    w = np.arange(WINDOW)
    ang = 2 * np.pi * ((w[:, None] * w[None, :]) % WINDOW) / WINDOW
    c, s = np.cos(ang), np.sin(ang)
    x = np.block([[c, -s], [s, c]])
    order = w.reshape(PARTS, fp, team).transpose(0, 2, 1).reshape(-1)
    y = np.concatenate([c[:, order], s[:, order]], axis=0)
    return a, host_split(b), host_split(x), host_split(y)


def split(x):
    hi = x.astype(bf16)
    return hi, (x - hi.astype(f32)).astype(bf16)


def dot(a, b):
    return jnp.dot(a, b, preferred_element_type=f32)


def dot_t(a, b):
    return lax.dot_general(a, b, (((1,), (1,)), ((), ())), preferred_element_type=f32)


def dot3(ah, al, bh, bl):
    return dot(ah, bh) + (dot(ah, bl) + dot(al, bh))


def kernel(n, team, chunk,
           t_hbm, beams_hbm, phases_hbm, pos_hbm, owner_hbm, a_hbm, bh_hbm, bl_hbm,
           xh_hbm, xl_hbm, yh_hbm, yl_hbm, out_ref,
           t_ref, beams_ref, phases_ref, pos_ref, owner_ref, a_ref, bh_ref, bl_ref,
           xh_ref, xl_ref, yh_ref, yl_ref, fetch,
           kmine, kbuf, th, tl, lh, ll, s_buf, eh, el, wh, wl, p_buf, xbuf, zbuf,
           ksend, krecv, xsend, xrecv):
    length = t_ref.shape[1]
    beams, probes = phases_ref.shape
    fold = WINDOW // team // PARTS
    hold = 2 * fold
    m = chunk * hold
    slots = team * CAP
    sj = slots * fold
    me = lax.axis_index("beam")
    mi = lax.rem(me, team)
    base = me - mi

    moves = [
        pltpu.make_async_copy(src, dst, fetch.at[i]) for i, (src, dst) in enumerate((
            (beams_hbm, beams_ref), (owner_hbm, owner_ref), (phases_hbm, phases_ref), (pos_hbm, pos_ref),
            (t_hbm, t_ref), (a_hbm.at[mi], a_ref), (bh_hbm, bh_ref), (bl_hbm, bl_ref),
            (xh_hbm, xh_ref), (xl_hbm, xl_ref), (yh_hbm, yh_ref), (yl_hbm, yl_ref)))]
    for move in moves:
        move.start()
    barrier = pltpu.get_barrier_semaphore()
    for d in range(1, n):
        pl.semaphore_signal(barrier, inc=1, device_id={"beam": lax.rem(me + d, n)}, device_id_type=MESH)
    moves[0].wait()
    half = lax.broadcasted_iota(jnp.int32, (8, 128), 0) < 4
    kmine[...] = jnp.where(half, beams_ref[0:1, 0:1], beams_ref[0:1, 1:2])
    kbuf[me] = kmine[...]
    pl.semaphore_wait(barrier, n - 1)
    sends = []
    for d in range(1, n):
        copy = pltpu.make_async_remote_copy(
            src_ref=kmine, dst_ref=kbuf.at[me], send_sem=ksend.at[d - 1], recv_sem=krecv.at[d - 1],
            device_id={"beam": lax.rem(me + d, n)}, device_id_type=MESH)
        copy.start()
        sends.append(copy)

    for move in moves[1:4]:
        move.wait()
    owner_row = owner_ref[...].astype(f32)
    pi = lax.broadcasted_iota(jnp.int32, (probes, probes), 0)
    pj = lax.broadcasted_iota(jnp.int32, (probes, probes), 1)
    owner_col = jnp.sum(jnp.where(pi == pj, owner_row, 0.0), axis=1, keepdims=True)
    rank = jnp.sum(jnp.where((owner_col == owner_row) & (pi < pj), 1.0, 0.0), axis=0, keepdims=True)
    target = owner_row * CAP + rank
    slot_id = (lax.broadcasted_iota(jnp.int32, (slots, probes), 0) + base * CAP).astype(f32)
    hit = jnp.where(target == slot_id, 1.0, 0.0)
    used = jnp.sum(hit, axis=1, keepdims=True)
    hit16 = hit.astype(bf16)
    place = dot_t(hit16, pos_ref[...].astype(f32).astype(bf16))
    level = dot_t(hit16, phases_ref[...].astype(f32).astype(bf16)).astype(bf16)

    def rows_of(x):
        return jnp.broadcast_to(x[:, None, :], (slots, fold, x.shape[-1])).reshape(sj, x.shape[-1])

    top = rows_of(jnp.broadcast_to(place[:, 0:1], (slots, 128)))[:, 0:1]
    left = rows_of(jnp.broadcast_to(place[:, 1:2], (slots, 128)))
    j_row = lax.broadcasted_iota(jnp.int32, (sj, 1), 0) & (fold - 1)
    scale = used * (1.0 / math.sqrt(beams))

    def weights(c):
        bi = lax.broadcasted_iota(jnp.int32, (beams, m), 0)
        bj = lax.broadcasted_iota(jnp.int32, (beams, m), 1)
        spread = jnp.where(bi == c * chunk + bj // hold, 1.0, 0.0).astype(bf16)
        angle = dot(level, spread) * (2.0 * math.pi / LEVELS)
        wc = rows_of(jnp.cos(angle) * scale)
        ws = rows_of(jnp.sin(angle) * scale)
        for h in range(PARTS):
            first = ((j_row + h * fold) * team + mi).astype(f32)
            pick = j_row + jnp.where(first < top, fold, 0)
            keep = (lax.broadcasted_iota(jnp.int32, (sj, m), 1) & (hold - 1)) == pick
            w_hi, w_lo = split(jnp.where(keep, wc, 0.0))
            wh[h, 0:sj] = w_hi
            wl[h, 0:sj] = w_lo
            w_hi, w_lo = split(jnp.where(keep, ws, 0.0))
            wh[h, sj:] = w_hi
            wl[h, sj:] = w_lo

    def waves(c):
        index = lax.broadcasted_iota(jnp.int32, (chunk, length), 1)
        out = []
        for row in (0, 4):
            k = kbuf[pl.ds(c * chunk, chunk), row, :]
            k = jnp.concatenate([k] * (length // 128), axis=1)
            ang = ((k * index) & (length - 1)).astype(f32) * (2.0 * math.pi / length)
            out += [jnp.cos(ang), jnp.sin(ang)]
        return out

    weights(0)

    moves[4].wait()
    t_hi, t_lo = split(t_ref[...])
    th[...] = t_hi
    tl[...] = t_lo
    for move in moves[5:]:
        move.wait()
    for copy in sends:
        copy.wait_recv()

    def one_chunk(h, wave, is_first):
        cy, sy, cx, sx = (v[:, None, :] for v in wave)
        ar = a_ref[h, 0][None]
        ai = a_ref[h, 1][None]
        lr_hi, lr_lo = split((ar * cy - ai * sy).reshape(m, length))
        li_hi, li_lo = split((ar * sy + ai * cy).reshape(m, length))
        lh[0:m, 0:length] = lr_hi
        ll[0:m, 0:length] = lr_lo
        lh[0:m, length:] = -li_hi
        ll[0:m, length:] = -li_lo
        lh[m:, 0:length] = li_hi
        ll[m:, 0:length] = li_lo
        lh[m:, length:] = lr_hi
        ll[m:, length:] = lr_lo

        @pl.loop(0, length // 256)
        def _(q):
            cols = pl.ds(pl.multiple_of(q * 256, 256), 256)
            s_buf[:, cols] = dot3(lh[...], ll[...], th[:, cols], tl[:, cols])

        sr = s_buf[0:m].reshape(chunk, hold, length)
        si = s_buf[m:].reshape(chunk, hold, length)
        hi, lo = split((sr * cx - si * sx).reshape(m, length))
        lh[0:m, 0:length] = hi
        ll[0:m, 0:length] = lo
        hi, lo = split((sr * sx + si * cx).reshape(m, length))
        lh[0:m, length:] = hi
        ll[0:m, length:] = lo

        @pl.loop(0, 2 * CROP // 256)
        def _(q):
            cols = pl.ds(pl.multiple_of(q * 256, 256), 256)
            hi, lo = split(dot3(lh[0:m], ll[0:m], bh_ref[:, cols], bl_ref[:, cols]))
            eh[:, cols] = hi
            el[:, cols] = lo

        @pl.loop(0, 2 * CROP // 256)
        def _(q):
            cols = pl.ds(pl.multiple_of(q * 256, 256), 256)
            part = dot3(wh[h], wl[h], eh[:, cols], el[:, cols])
            p_buf[:, cols] = part if is_first else p_buf[:, cols] + part

    copies = []
    wave = waves(0)
    for h in range(PARTS):
        if beams > chunk and h > 0:
            weights(0)
        one_chunk(h, wave, True)
        if beams > chunk:
            @pl.loop(1, beams // chunk)
            def _(c):
                weights(c)
                one_chunk(h, waves(c), False)

        vr = p_buf[0:sj, 0:CROP] - p_buf[sj:, CROP:]
        vi = p_buf[0:sj, CROP:] + p_buf[sj:, 0:CROP]
        inside = lax.broadcasted_iota(jnp.int32, (sj, WINDOW), 1).astype(f32) >= left
        folded = jnp.concatenate(
            [jnp.where(inside, vr[:, 0:WINDOW], vr[:, WINDOW:]),
             jnp.where(inside, vi[:, 0:WINDOW], vi[:, WINDOW:])], axis=1)
        f_hi, f_lo = split(folded)
        xbuf[h] = dot3(f_hi, f_lo, xh_ref[...], xl_ref[...]).reshape(team, CAP * fold, 2 * WINDOW)
        for e in range(1, team):
            other = lax.rem(mi + e, team)
            at = h * (team - 1) + e - 1
            copy = pltpu.make_async_remote_copy(
                src_ref=xbuf.at[h, other], dst_ref=zbuf.at[h, mi], send_sem=xsend.at[at], recv_sem=xrecv.at[at],
                device_id={"beam": base + other}, device_id_type=MESH)
            copy.start()
            copies.append(copy)
        zbuf[h, mi] = xbuf[h, mi]
    for copy in copies:
        copy.wait_recv()
    for k in range(CAP):
        z = zbuf[:, :, k * fold:(k + 1) * fold, :].reshape(WINDOW, 2 * WINDOW)
        z_hi, z_lo = split(z)
        y = dot3(yh_ref[...], yl_ref[...], z_hi, z_lo)
        yr = y[0:WINDOW, 0:WINDOW] + y[WINDOW:, WINDOW:]
        yi = y[0:WINDOW, WINDOW:] - y[WINDOW:, 0:WINDOW]
        out_ref[k] = (yr * yr + yi * yi) * (1.0 / (WINDOW * WINDOW))
    for copy in sends + copies:
        copy.wait_send()


def solution(mesh):
    n = mesh.shape["beam"]
    team = math.gcd(n, TEAM)

    def local(transmission, beams, phases, positions, owner):
        length = transmission.shape[-1]
        probes, beam_total = phases.shape
        chunk = math.gcd(beam_total, CHUNK)
        a, b, x, y = constants(length, team)
        m = chunk * (CROP // team // PARTS)
        sj = CAP * WINDOW // PARTS
        t = transmission.reshape(2 * length, length)
        operands = (t, beams, phases.T, positions.T, owner.reshape(1, probes), a, *b, *x, *y)
        held = [pltpu.VMEM(v.shape[1:] if v is a else v.shape, v.dtype) for v in operands]
        return pl.pallas_call(
            functools.partial(kernel, n, team, chunk),
            out_shape=jax.ShapeDtypeStruct((CAP, WINDOW, WINDOW), f32),
            in_specs=[pl.BlockSpec(memory_space=pl.ANY)] * 12,
            out_specs=pl.BlockSpec(memory_space=pltpu.VMEM),
            scratch_shapes=held + [
                pltpu.SemaphoreType.DMA((len(operands),)),
                pltpu.VMEM((8, 128), jnp.int32),
                pltpu.VMEM((n, 8, 128), jnp.int32),
                pltpu.VMEM((2 * length, length), bf16),
                pltpu.VMEM((2 * length, length), bf16),
                pltpu.VMEM((2 * m, 2 * length), bf16),
                pltpu.VMEM((2 * m, 2 * length), bf16),
                pltpu.VMEM((2 * m, length), f32),
                pltpu.VMEM((m, 2 * CROP), bf16),
                pltpu.VMEM((m, 2 * CROP), bf16),
                pltpu.VMEM((PARTS, 2 * sj, m), bf16),
                pltpu.VMEM((PARTS, 2 * sj, m), bf16),
                pltpu.VMEM((2 * sj, 2 * CROP), f32),
                pltpu.VMEM((PARTS, team, CAP * WINDOW // team // PARTS, 2 * WINDOW), f32),
                pltpu.VMEM((PARTS, team, CAP * WINDOW // team // PARTS, 2 * WINDOW), f32),
                pltpu.SemaphoreType.DMA((n - 1,)),
                pltpu.SemaphoreType.DMA((n - 1,)),
                pltpu.SemaphoreType.DMA((PARTS * (team - 1),)),
                pltpu.SemaphoreType.DMA((PARTS * (team - 1),)),
            ],
            compiler_params=pltpu.CompilerParams(
                collective_id=0, has_side_effects=True, vmem_limit_bytes=60 << 20),
        )(*operands)

    in_specs = (P("groups", None, None, None), P("beam", None), P(), P(), P())
    out_specs = P(("groups", "beam"), None, None)
    return jax.shard_map(local, mesh=mesh, in_specs=in_specs, out_specs=out_specs, check_vma=False)
```

```python
import functools
import math

import jax
import jax.numpy as jnp
import ml_dtypes
import numpy as np
from jax import lax
from jax.experimental import pallas as pl
from jax.experimental.pallas import tpu as pltpu
from jax.sharding import PartitionSpec as P

GRID = 512
CROP = 256
WINDOW = 128
LEVELS = 64
CAP = 4
TEAM = 8
CHUNK = 16
PARTS = 2

bf16 = jnp.bfloat16
f32 = jnp.float32
MESH = pl.DeviceIdType.MESH


def host_split(x):
    x = np.asarray(x, np.float32)
    hi = x.astype(ml_dtypes.bfloat16)
    lo = (x - hi.astype(np.float32)).astype(ml_dtypes.bfloat16)
    return hi, lo


def constants(length, team):
    index = np.arange(length)
    freq = np.where(index < length // 2, index, index - length)
    chirp = np.exp(-1j * 0.0004 * np.pi * freq.astype(np.float64) ** 2)
    kernel = np.fft.ifft(chirp)
    rows = (length - CROP) // 2 + np.arange(CROP)
    step = kernel[(rows[:, None] - index[None, :]) % length]
    fp = WINDOW // team // PARTS
    dealt = step.reshape(2, PARTS, fp, team, length).transpose(3, 1, 0, 2, 4).reshape(team, PARTS, 2 * fp, length)
    a = np.stack([dealt.real, dealt.imag], axis=2).astype(np.float32)
    st = step.T
    b = np.block([[st.real, st.imag], [-st.imag, st.real]])
    w = np.arange(WINDOW)
    ang = 2 * np.pi * ((w[:, None] * w[None, :]) % WINDOW) / WINDOW
    c, s = np.cos(ang), np.sin(ang)
    x = np.block([[c, -s], [s, c]])
    order = w.reshape(PARTS, fp, team).transpose(0, 2, 1).reshape(-1)
    y = np.concatenate([c[:, order], s[:, order]], axis=0)
    return a, host_split(b), host_split(x), host_split(y)


def split(x):
    hi = x.astype(bf16)
    return hi, (x - hi.astype(f32)).astype(bf16)


def dot(a, b):
    return jnp.dot(a, b, preferred_element_type=f32)


def dot_t(a, b):
    return lax.dot_general(a, b, (((1,), (1,)), ((), ())), preferred_element_type=f32)


def turn(q, n):
    e = n // 8
    up = q + e
    quad = (up >> (n // 4).bit_length() - 1) & 3
    x = ((up & (n // 4 - 1)) - e).astype(f32) * (2.0 * math.pi / n)
    x2 = x * x
    s = x * (1.0 + x2 * (-1 / 6 + x2 * (1 / 120 + x2 * (-1 / 5040 + x2 * (1 / 362880)))))
    c = 1.0 + x2 * (-1 / 2 + x2 * (1 / 24 + x2 * (-1 / 720 + x2 * (1 / 40320))))
    odd = (quad & 1) == 1
    cos = jnp.where(odd, s, c)
    sin = jnp.where(odd, c, s)
    return jnp.where(((quad + 1) & 2) == 2, -cos, cos), jnp.where(quad >= 2, -sin, sin)


def dot3(ah, al, bh, bl):
    return dot(ah, bh) + (dot(ah, bl) + dot(al, bh))


def kernel(n, team, chunk,
           t_hbm, beams_hbm, phases_hbm, pos_hbm, owner_hbm, a_hbm, bh_hbm, bl_hbm,
           xh_hbm, xl_hbm, yh_hbm, yl_hbm, out_ref,
           t_ref, beams_ref, phases_ref, pos_ref, owner_ref, a_ref, bh_ref, bl_ref,
           xh_ref, xl_ref, yh_ref, yl_ref, fetch,
           kmine, kbuf, th, tl, lh, ll, s_buf, eh, el, wh, wl, p_buf, xbuf, zbuf,
           ksend, krecv, xsend, xrecv):
    length = t_ref.shape[1]
    beams, probes = phases_ref.shape
    fold = WINDOW // team // PARTS
    hold = 2 * fold
    m = chunk * hold
    slots = team * CAP
    sj = slots * fold
    me = lax.axis_index("beam")
    mi = lax.rem(me, team)
    base = me - mi

    moves = [
        pltpu.make_async_copy(src, dst, fetch.at[i]) for i, (src, dst) in enumerate((
            (beams_hbm, beams_ref), (owner_hbm, owner_ref), (phases_hbm, phases_ref), (pos_hbm, pos_ref),
            (t_hbm, t_ref), (a_hbm.at[mi], a_ref), (bh_hbm, bh_ref), (bl_hbm, bl_ref),
            (xh_hbm, xh_ref), (xl_hbm, xl_ref), (yh_hbm, yh_ref), (yl_hbm, yl_ref)))]
    for move in moves:
        move.start()
    barrier = pltpu.get_barrier_semaphore()
    for d in range(1, n):
        pl.semaphore_signal(barrier, inc=1, device_id={"beam": lax.rem(me + d, n)}, device_id_type=MESH)
    moves[0].wait()
    half = lax.broadcasted_iota(jnp.int32, (8, 128), 0) < 4
    kmine[...] = jnp.where(half, beams_ref[0:1, 0:1], beams_ref[0:1, 1:2])
    kbuf[me] = kmine[...]
    pl.semaphore_wait(barrier, n - 1)
    sends = []
    for d in range(1, n):
        copy = pltpu.make_async_remote_copy(
            src_ref=kmine, dst_ref=kbuf.at[me], send_sem=ksend.at[d - 1], recv_sem=krecv.at[d - 1],
            device_id={"beam": lax.rem(me + d, n)}, device_id_type=MESH)
        copy.start()
        sends.append(copy)

    for move in moves[1:4]:
        move.wait()
    owner_row = owner_ref[...].astype(f32)
    pi = lax.broadcasted_iota(jnp.int32, (probes, probes), 0)
    pj = lax.broadcasted_iota(jnp.int32, (probes, probes), 1)
    owner_col = jnp.sum(jnp.where(pi == pj, owner_row, 0.0), axis=1, keepdims=True)
    rank = jnp.sum(jnp.where((owner_col == owner_row) & (pi < pj), 1.0, 0.0), axis=0, keepdims=True)
    target = owner_row * CAP + rank
    slot_id = (lax.broadcasted_iota(jnp.int32, (slots, probes), 0) + base * CAP).astype(f32)
    hit = jnp.where(target == slot_id, 1.0, 0.0)
    used = jnp.sum(hit, axis=1, keepdims=True)
    hit16 = hit.astype(bf16)
    place = dot_t(hit16, pos_ref[...].astype(f32).astype(bf16))
    level = dot_t(hit16, phases_ref[...].astype(f32).astype(bf16)).astype(bf16)

    def rows_of(x):
        return jnp.broadcast_to(x[:, None, :], (slots, fold, x.shape[-1])).reshape(sj, x.shape[-1])

    top = rows_of(jnp.broadcast_to(place[:, 0:1], (slots, 128)))[:, 0:1]
    left = rows_of(jnp.broadcast_to(place[:, 1:2], (slots, 128)))
    j_row = lax.broadcasted_iota(jnp.int32, (sj, 1), 0) & (fold - 1)
    scale = used * (1.0 / math.sqrt(beams))

    def weights(c):
        bi = lax.broadcasted_iota(jnp.int32, (beams, m), 0)
        bj = lax.broadcasted_iota(jnp.int32, (beams, m), 1)
        spread = jnp.where(bi == c * chunk + bj // hold, 1.0, 0.0).astype(bf16)
        cos, sin = turn(dot(level, spread).astype(jnp.int32), LEVELS)
        wc = rows_of(cos * scale)
        ws = rows_of(sin * scale)
        for h in range(PARTS):
            first = ((j_row + h * fold) * team + mi).astype(f32)
            pick = j_row + jnp.where(first < top, fold, 0)
            keep = (lax.broadcasted_iota(jnp.int32, (sj, m), 1) & (hold - 1)) == pick
            w_hi, w_lo = split(jnp.where(keep, wc, 0.0))
            wh[h, 0:sj] = w_hi
            wl[h, 0:sj] = w_lo
            w_hi, w_lo = split(jnp.where(keep, ws, 0.0))
            wh[h, sj:] = w_hi
            wl[h, sj:] = w_lo

    def waves(c):
        index = lax.broadcasted_iota(jnp.int32, (chunk, length), 1)
        out = []
        for row in (0, 4):
            k = kbuf[pl.ds(c * chunk, chunk), row, :]
            k = jnp.concatenate([k] * (length // 128), axis=1)
            out += turn((k * index) & (length - 1), length)
        return out

    weights(0)

    moves[4].wait()
    t_hi, t_lo = split(t_ref[...])
    th[...] = t_hi
    tl[...] = t_lo
    for move in moves[5:]:
        move.wait()
    for copy in sends:
        copy.wait_recv()

    def one_chunk(h, wave, is_first):
        cy, sy, cx, sx = (v[:, None, :] for v in wave)
        ar = a_ref[h, 0][None]
        ai = a_ref[h, 1][None]
        lr_hi, lr_lo = split((ar * cy - ai * sy).reshape(m, length))
        li_hi, li_lo = split((ar * sy + ai * cy).reshape(m, length))
        lh[0:m, 0:length] = lr_hi
        ll[0:m, 0:length] = lr_lo
        lh[0:m, length:] = -li_hi
        ll[0:m, length:] = -li_lo
        lh[m:, 0:length] = li_hi
        ll[m:, 0:length] = li_lo
        lh[m:, length:] = lr_hi
        ll[m:, length:] = lr_lo

        for q in range(length // 256):
            cols = slice(q * 256, q * 256 + 256)
            s_buf[:, cols] = dot3(lh[...], ll[...], th[:, cols], tl[:, cols])

        sr = s_buf[0:m].reshape(chunk, hold, length)
        si = s_buf[m:].reshape(chunk, hold, length)
        hi, lo = split((sr * cx - si * sx).reshape(m, length))
        lh[0:m, 0:length] = hi
        ll[0:m, 0:length] = lo
        hi, lo = split((sr * sx + si * cx).reshape(m, length))
        lh[0:m, length:] = hi
        ll[0:m, length:] = lo

        for q in range(2 * CROP // 256):
            cols = slice(q * 256, q * 256 + 256)
            hi, lo = split(dot3(lh[0:m], ll[0:m], bh_ref[:, cols], bl_ref[:, cols]))
            eh[:, cols] = hi
            el[:, cols] = lo

        for q in range(2 * CROP // 256):
            cols = slice(q * 256, q * 256 + 256)
            part = dot3(wh[h], wl[h], eh[:, cols], el[:, cols])
            p_buf[:, cols] = part if is_first else p_buf[:, cols] + part

    copies = []
    wave = waves(0)
    for h in range(PARTS):
        if beams > chunk and h > 0:
            weights(0)
        one_chunk(h, wave, True)
        if beams > chunk:
            @pl.loop(1, beams // chunk)
            def _(c):
                weights(c)
                one_chunk(h, waves(c), False)

        vr = p_buf[0:sj, 0:CROP] - p_buf[sj:, CROP:]
        vi = p_buf[0:sj, CROP:] + p_buf[sj:, 0:CROP]
        inside = lax.broadcasted_iota(jnp.int32, (sj, WINDOW), 1).astype(f32) >= left
        folded = jnp.concatenate(
            [jnp.where(inside, vr[:, 0:WINDOW], vr[:, WINDOW:]),
             jnp.where(inside, vi[:, 0:WINDOW], vi[:, WINDOW:])], axis=1)
        f_hi, f_lo = split(folded)
        xbuf[h] = dot3(f_hi, f_lo, xh_ref[...], xl_ref[...]).reshape(team, CAP * fold, 2 * WINDOW)
        for e in range(1, team):
            other = lax.rem(mi + e, team)
            at = h * (team - 1) + e - 1
            copy = pltpu.make_async_remote_copy(
                src_ref=xbuf.at[h, other], dst_ref=zbuf.at[h, mi], send_sem=xsend.at[at], recv_sem=xrecv.at[at],
                device_id={"beam": base + other}, device_id_type=MESH)
            copy.start()
            copies.append(copy)
        zbuf[h, mi] = xbuf[h, mi]
    for copy in copies:
        copy.wait_recv()
    for k in range(CAP):
        z = zbuf[:, :, k * fold:(k + 1) * fold, :].reshape(WINDOW, 2 * WINDOW)
        z_hi, z_lo = split(z)
        y = dot3(yh_ref[...], yl_ref[...], z_hi, z_lo)
        yr = y[0:WINDOW, 0:WINDOW] + y[WINDOW:, WINDOW:]
        yi = y[0:WINDOW, WINDOW:] - y[WINDOW:, 0:WINDOW]
        out_ref[k] = (yr * yr + yi * yi) * (1.0 / (WINDOW * WINDOW))
    for copy in sends + copies:
        copy.wait_send()


def solution(mesh):
    n = mesh.shape["beam"]
    team = math.gcd(n, TEAM)

    def local(transmission, beams, phases, positions, owner):
        length = transmission.shape[-1]
        probes, beam_total = phases.shape
        chunk = math.gcd(beam_total, CHUNK)
        a, b, x, y = constants(length, team)
        m = chunk * (CROP // team // PARTS)
        sj = CAP * WINDOW // PARTS
        t = transmission.reshape(2 * length, length)
        operands = (t, beams, phases.T, positions.T, owner.reshape(1, probes), a, *b, *x, *y)
        held = [pltpu.VMEM(v.shape[1:] if v is a else v.shape, v.dtype) for v in operands]
        return pl.pallas_call(
            functools.partial(kernel, n, team, chunk),
            out_shape=jax.ShapeDtypeStruct((CAP, WINDOW, WINDOW), f32),
            in_specs=[pl.BlockSpec(memory_space=pl.ANY)] * 12,
            out_specs=pl.BlockSpec(memory_space=pltpu.VMEM),
            scratch_shapes=held + [
                pltpu.SemaphoreType.DMA((len(operands),)),
                pltpu.VMEM((8, 128), jnp.int32),
                pltpu.VMEM((n, 8, 128), jnp.int32),
                pltpu.VMEM((2 * length, length), bf16),
                pltpu.VMEM((2 * length, length), bf16),
                pltpu.VMEM((2 * m, 2 * length), bf16),
                pltpu.VMEM((2 * m, 2 * length), bf16),
                pltpu.VMEM((2 * m, length), f32),
                pltpu.VMEM((m, 2 * CROP), bf16),
                pltpu.VMEM((m, 2 * CROP), bf16),
                pltpu.VMEM((PARTS, 2 * sj, m), bf16),
                pltpu.VMEM((PARTS, 2 * sj, m), bf16),
                pltpu.VMEM((2 * sj, 2 * CROP), f32),
                pltpu.VMEM((PARTS, team, CAP * WINDOW // team // PARTS, 2 * WINDOW), f32),
                pltpu.VMEM((PARTS, team, CAP * WINDOW // team // PARTS, 2 * WINDOW), f32),
                pltpu.SemaphoreType.DMA((n - 1,)),
                pltpu.SemaphoreType.DMA((n - 1,)),
                pltpu.SemaphoreType.DMA((PARTS * (team - 1),)),
                pltpu.SemaphoreType.DMA((PARTS * (team - 1),)),
            ],
            compiler_params=pltpu.CompilerParams(
                collective_id=0, has_side_effects=True, vmem_limit_bytes=60 << 20),
        )(*operands)

    in_specs = (P("groups", None, None, None), P("beam", None), P(), P(), P())
    out_specs = P(("groups", "beam"), None, None)
    return jax.shard_map(local, mesh=mesh, in_specs=in_specs, out_specs=out_specs, check_vma=False)
```
